32 devices in a mesh: parts: 2 (over y), blk: 4 (over z), dim: 2 (over x), qs: 2 (over core).
Axes of the slice: x: 2, y: 2, z: 4, core: 2. Of those that a mesh axis runs over, the one named last changes fastest.
Arguments:
- train_grads: bfloat16 [1024, 65536], P(('parts', 'blk'), 'dim'), parts along dimension 0, may hold values from -6 to 6
- query_grads: bfloat16 [1024, 65536], P(('parts', 'blk', 'qs'), 'dim'), parts along dimension 0, may hold values from -0.0078125 to 0.0078125
- fisher: float32 [65536], P('dim'), may hold values from 0.05 to 5
- train_ids: int32 [1024], P(('parts', 'blk', 'dim')), parts along dimension 0, may hold values from 0 to 15
- query_ids: int32 [1024], P('parts'), parts along dimension 0, may hold values from 0 to 15
Outputs:
- scores: float32 [1024, 256], P(('parts', 'blk', 'dim'), 'qs'), parts along dimension 0
The draws below stay inside these ranges and needn't reach their ends.
There are 2 independent parts, one for each index of `parts`. The reference program is written for one: setup_inputs(seed, part) draws one part's arguments, and reference() takes and returns one part's arrays. A program takes and returns all parts, laid end to end along the dimension named above; an argument that names none is the same for every part. Nothing has to cross between parts.
All inputs are finite; a program needn't handle non-finite values.
Results may differ from the reference program's by a relative error of at most 0.0029.
Values may be sent and summed in bfloat16 or wider, within the bound.
A program may use at most 64 MiB of HBM per device.

```python
import math
import jax
import jax.numpy as jnp
from jax import lax

K = 65536
TR_DEV = 128
QB = 64
STEPS = 2
CLUSTERS = 16
NBLK = 4
NQS = 2
TRAIN = 512
QUERIES = 512
QWIN = 256


def place_ends(entries, stream_key, smallest, high):
    spot = [jax.random.randint(jax.random.fold_in(stream_key, axis), (), 0, length) for axis, length in enumerate(entries.shape)]
    longest = entries.shape.index(max(entries.shape))
    next_to = spot[:longest] + [(spot[longest] + 1) % entries.shape[longest]] + spot[longest + 1:]
    return entries.at[tuple(spot)].set(smallest).at[tuple(next_to)].set(high)


def level_of(own_key, dims, shards, smallest, top_value):
    factor_of = 1.0
    for dim, parts in shards:
        heights = jax.random.uniform(jax.random.fold_in(jax.random.fold_in(own_key, 6), dim), (parts,), jnp.float32, smallest / len(shards), top_value / len(shards))
        factor_of = factor_of * jnp.repeat(jnp.exp(heights), dims[dim] // parts).reshape((-1,) + (1,) * (len(dims) - 1 - dim))
    return factor_of


def gaussian(stream_key, dims, spread, reach, shards=(), held_as=jnp.bfloat16):
    entries = spread * jax.random.normal(stream_key, dims, jnp.float32)
    if shards:
        entries = entries * level_of(stream_key, dims, shards, -0.22, 0.18)
    return jnp.clip(entries, -reach, reach).astype(held_as)


def setup_inputs(seed: int = 0, part: int = 0) -> dict:
    arg_keys = jax.random.split(jax.random.key(seed), 6)
    part_splits = jax.random.split(jax.random.fold_in(arg_keys[5], part), 6)
    return {
        "train_grads": gaussian(part_splits[0], (TRAIN, K), 1.0, 6.0, ((0, 4), (1, 2))),
        "query_grads": gaussian(part_splits[1], (QUERIES, K), (8 * K) ** -0.5, 0.0078125, ((0, 8), (1, 2))),
        "fisher": jnp.clip(jnp.exp(math.log(5.0) - 4.6051702 * jax.random.uniform(arg_keys[2], (K,), jnp.float32) ** level_of(arg_keys[2], (K,), ((0, 2),), -0.2, 0.2)), 0.05, 5.0),
        "train_ids": place_ends(jax.random.randint(part_splits[3], (TRAIN,), 0, CLUSTERS), jax.random.fold_in(part_splits[3], 1), 0, CLUSTERS - 1).astype(jnp.int32),
        "query_ids": place_ends(jax.random.randint(part_splits[4], (QUERIES,), 0, CLUSTERS), jax.random.fold_in(part_splits[4], 1), 0, CLUSTERS - 1).astype(jnp.int32),
    }


damping = 0.1


def reference(train_grads, query_grads, fisher, train_ids, query_ids):
    scaled = (query_grads.astype(jnp.float32) / (fisher + damping)).astype(jnp.bfloat16)
    group_rows = NQS * QB

    def one_group(group_index):
        first_row = (group_index * TR_DEV).astype(jnp.int32)
        train_rows = lax.dynamic_slice_in_dim(train_grads, first_row, TR_DEV, 0)
        train_keys = lax.dynamic_slice_in_dim(train_ids, first_row, TR_DEV, 0)
        columns = []
        for offset in range(STEPS):
            source = (((group_index - offset) % NBLK) * group_rows).astype(jnp.int32)
            query_rows = lax.dynamic_slice_in_dim(scaled, source, group_rows, 0)
            query_keys = lax.dynamic_slice_in_dim(query_ids, source, group_rows, 0)
            tile_scores = jnp.dot(train_rows, query_rows.T, preferred_element_type=jnp.float32)
            tile_scores = jnp.where(train_keys[:, None] == query_keys[None, :], jnp.zeros_like(tile_scores), tile_scores)
            columns.append(tile_scores.reshape(TR_DEV, NQS, 1, QB))
        return jnp.concatenate(columns, axis=2).reshape(TR_DEV, QWIN)

    result = lax.map(one_group, jnp.arange(NBLK, dtype=jnp.int32))
    return result.reshape(TRAIN, QWIN)
```

```python
import functools

import jax
import jax.numpy as jnp
from jax import lax
from jax.experimental import pallas as pl
from jax.experimental.pallas import tpu as pltpu
from jax.sharding import PartitionSpec as P

STEPS = 2
DAMPING = 0.1
CHUNK = 2048
IN_FLIGHT = 4
MESH = pl.DeviceIdType.MESH


def kernel(sizes, train_hbm, query_hbm, fisher_hbm, train_ids_hbm, query_ids_hbm, out_ref,
           train, own, inbox, scale, train_ids, query_ids, partial, peers,
           send_sem, recv_sem, load_sem, peer_send_sem, peer_recv_sem):
    cycle, dims, halves = sizes
    blk = lax.axis_index("blk")
    dim = lax.axis_index("dim")
    half = lax.axis_index("qs")
    after = lax.rem(blk + 1, cycle)
    before = lax.rem(blk + cycle - 1, cycle)
    train_rows = train.shape[0]
    query_rows, depth = own.shape
    owned = train_rows // dims
    chunks = depth // CHUNK

    def peer(k):
        return lax.rem(dim + k, dims)

    barrier = pltpu.get_barrier_semaphore()
    pl.semaphore_signal(barrier, inc=1, device_id={"blk": before}, device_id_type=MESH)
    for k in range(1, dims):
        pl.semaphore_signal(barrier, inc=1, device_id={"dim": peer(k)}, device_id_type=MESH)
    pl.semaphore_wait(barrier, dims)

    def transfer(i):
        return pltpu.make_async_remote_copy(
            src_ref=query_hbm.at[:, pl.ds(pl.multiple_of(i * CHUNK, CHUNK), CHUNK)],
            dst_ref=inbox.at[i],
            send_sem=send_sem.at[i],
            recv_sem=recv_sem.at[i],
            device_id={"blk": after},
            device_id_type=MESH,
        )

    flight = min(IN_FLIGHT, chunks)
    for i in range(flight):
        transfer(i).start()

    loads = [
        pltpu.make_async_copy(source, target, load_sem.at[n])
        for n, (source, target) in enumerate([
            (fisher_hbm, scale), (query_hbm, own), (train_hbm, train),
            (train_ids_hbm, train_ids), (query_ids_hbm, query_ids)])
    ]
    for load in loads:
        load.start()
    for load in loads:
        load.wait()

    scale[...] = 1.0 / (scale[...] + DAMPING)

    def score(columns, rows, total):
        scaled = (rows.astype(jnp.float32) * scale[:, columns]).astype(jnp.bfloat16)
        return total + lax.dot_general(
            train[:, columns], scaled, (((1,), (1,)), ((), ())), preferred_element_type=jnp.float32)

    def columns_of(i):
        return pl.ds(pl.multiple_of(i * CHUNK, CHUNK), CHUNK)

    zero = jnp.zeros((train_rows, query_rows), jnp.float32)

    def own_step(i, total):
        columns = columns_of(i)
        return score(columns, own[:, columns], total)

    def exchange(step):
        copies = []
        for k in range(1, dims):
            copies.append(pltpu.make_async_remote_copy(
                src_ref=partial.at[step, pl.ds(pl.multiple_of(peer(k) * owned, owned), owned)],
                dst_ref=peers.at[step, k - 1],
                send_sem=peer_send_sem.at[step, k - 1],
                recv_sem=peer_recv_sem.at[step, k - 1],
                device_id={"dim": peer(k)},
                device_id_type=MESH,
            ))
        for copy in copies:
            copy.start()
        return copies

    partial[0] = lax.fori_loop(0, chunks, own_step, zero)
    first = exchange(0)

    def same_cluster():
        row = train_ids[...].astype(jnp.float32)
        diagonal = (lax.broadcasted_iota(jnp.int32, (owned, owned), 0)
                    == lax.broadcasted_iota(jnp.int32, (owned, owned), 1))
        column = jnp.sum(jnp.where(diagonal, jnp.broadcast_to(row, (owned, owned)), 0.0), axis=1, keepdims=True)
        equal = []
        for step in range(STEPS):
            group = halves * query_rows
            source = lax.rem(blk + cycle - step, cycle)
            both = query_ids[:, pl.ds(pl.multiple_of(source * group, group), group)].astype(jnp.float32)
            keys = both[:, :query_rows]
            for h in range(1, halves):
                keys = jnp.where(half == h, both[:, h * query_rows:(h + 1) * query_rows], keys)
            equal.append(jnp.broadcast_to(column, (owned, query_rows)) == jnp.broadcast_to(keys, (owned, query_rows)))
        return equal

    equal = same_cluster()
    mine = pl.ds(pl.multiple_of(dim * owned, owned), owned)

    def finish(step, copies):
        total = partial[step, mine]
        for k, copy in enumerate(copies):
            copy.wait_recv()
            total = total + peers[step, k]
        out_ref[:, step * query_rows:(step + 1) * query_rows] = jnp.where(equal[step], 0.0, total)

    finish(0, first)

    def next_step(i, total):
        transfer(i).wait_send()

        @pl.when(i + flight < chunks)
        def _():
            transfer(i + flight).start()

        transfer(i).wait_recv()
        return score(columns_of(i), inbox[i], total)

    partial[1] = lax.fori_loop(0, chunks, next_step, zero)
    second = exchange(1)
    finish(1, second)
    for copy in first + second:
        copy.wait_send()


def solution(mesh):
    sizes = (mesh.shape["blk"], mesh.shape["dim"], mesh.shape["qs"])
    dims = sizes[1]

    def on_device(train_grads, query_grads, fisher, train_ids, query_ids):
        train_rows, depth = train_grads.shape
        query_rows = query_grads.shape[0]
        owned = train_ids.shape[0]
        chunks = depth // CHUNK
        out_shape = jax.ShapeDtypeStruct((owned, STEPS * query_rows), jnp.float32)
        return pl.pallas_call(
            functools.partial(kernel, sizes),
            out_shape=out_shape,
            in_specs=[pl.BlockSpec(memory_space=pltpu.HBM)] * 5,
            out_specs=pl.BlockSpec(memory_space=pltpu.VMEM),
            scratch_shapes=[
                pltpu.VMEM((train_rows, depth), train_grads.dtype),
                pltpu.VMEM((query_rows, depth), query_grads.dtype),
                pltpu.VMEM((chunks, query_rows, CHUNK), query_grads.dtype),
                pltpu.VMEM((1, depth), jnp.float32),
                pltpu.VMEM((1, owned), jnp.int32),
                pltpu.VMEM((1, query_ids.shape[0]), jnp.int32),
                pltpu.VMEM((STEPS, train_rows, query_rows), jnp.float32),
                pltpu.VMEM((STEPS, max(dims - 1, 1), owned, query_rows), jnp.float32),
                pltpu.SemaphoreType.DMA((chunks,)),
                pltpu.SemaphoreType.DMA((chunks,)),
                pltpu.SemaphoreType.DMA((5,)),
                pltpu.SemaphoreType.DMA((STEPS, max(dims - 1, 1))),
                pltpu.SemaphoreType.DMA((STEPS, max(dims - 1, 1))),
            ],
            cost_estimate=pl.CostEstimate(
                flops=4 * train_rows * query_rows * depth,
                bytes_accessed=2 * depth * (train_rows + 2 * query_rows), transcendentals=0),
            compiler_params=pltpu.CompilerParams(
                collective_id=0, has_side_effects=True, vmem_limit_bytes=48 << 20),
        )(train_grads, query_grads, fisher.reshape(1, -1), train_ids.reshape(1, -1), query_ids.reshape(1, -1))

    return jax.shard_map(
        on_device,
        mesh=mesh,
        in_specs=(
            P(("parts", "blk"), "dim"),
            P(("parts", "blk", "qs"), "dim"),
            P("dim"),
            P(("parts", "blk", "dim")),
            P("parts"),
        ),
        out_specs=P(("parts", "blk", "dim"), "qs"),
        check_vma=False,
    )
```

```python
import functools

import jax
import jax.numpy as jnp
from jax import lax
from jax.experimental import pallas as pl
from jax.experimental.pallas import tpu as pltpu
from jax.sharding import PartitionSpec as P

STEPS = 2
DAMPING = 0.1
CHUNK = 2048
IN_FLIGHT = 4
MESH = pl.DeviceIdType.MESH


def kernel(sizes, train_hbm, query_hbm, fisher_hbm, train_ids_hbm, query_ids_hbm, out_ref,
           train, own, inbox, scale, train_ids, query_ids, partial, peers,
           send_sem, recv_sem, load_sem, peer_send_sem, peer_recv_sem):
    cycle, dims, halves = sizes
    blk = lax.axis_index("blk")
    dim = lax.axis_index("dim")
    half = lax.axis_index("qs")
    after = lax.rem(blk + 1, cycle)
    before = lax.rem(blk + cycle - 1, cycle)
    train_rows = train.shape[0]
    query_rows, depth = own.shape
    owned = train_rows // dims
    chunks = depth // CHUNK

    def peer(k):
        return lax.rem(dim + k, dims)

    barrier = pltpu.get_barrier_semaphore()
    pl.semaphore_signal(barrier, inc=1, device_id={"blk": before}, device_id_type=MESH)
    for k in range(1, dims):
        pl.semaphore_signal(barrier, inc=1, device_id={"dim": peer(k)}, device_id_type=MESH)
    pl.semaphore_wait(barrier, dims)

    def transfer(i):
        return pltpu.make_async_remote_copy(
            src_ref=query_hbm.at[:, pl.ds(pl.multiple_of(i * CHUNK, CHUNK), CHUNK)],
            dst_ref=inbox.at[i],
            send_sem=send_sem.at[i],
            recv_sem=recv_sem.at[i],
            device_id={"blk": after},
            device_id_type=MESH,
        )

    flight = min(IN_FLIGHT, chunks)
    for i in range(flight):
        transfer(i).start()

    loads = [
        pltpu.make_async_copy(source, target, load_sem.at[n])
        for n, (source, target) in enumerate([
            (fisher_hbm, scale), (query_hbm, own), (train_hbm, train),
            (train_ids_hbm, train_ids), (query_ids_hbm, query_ids)])
    ]
    for load in loads:
        load.start()
    for load in loads:
        load.wait()

    scale[...] = 1.0 / (scale[...] + DAMPING)

    def score(columns, rows, total):
        scaled = (rows.astype(jnp.float32) * scale[:, columns]).astype(jnp.bfloat16)
        return total + lax.dot_general(
            train[:, columns], scaled, (((1,), (1,)), ((), ())), preferred_element_type=jnp.float32)

    def columns_of(i):
        return pl.ds(pl.multiple_of(i * CHUNK, CHUNK), CHUNK)

    zero = jnp.zeros((train_rows, query_rows), jnp.float32)

    def own_step(i, total):
        columns = columns_of(i)
        return score(columns, own[:, columns], total)

    def exchange(step):
        copies = []
        for k in range(1, dims):
            copies.append(pltpu.make_async_remote_copy(
                src_ref=partial.at[step, pl.ds(pl.multiple_of(peer(k) * owned, owned), owned)],
                dst_ref=peers.at[step, k - 1],
                send_sem=peer_send_sem.at[step, k - 1],
                recv_sem=peer_recv_sem.at[step, k - 1],
                device_id={"dim": peer(k)},
                device_id_type=MESH,
            ))
        for copy in copies:
            copy.start()
        return copies

    partial[0] = lax.fori_loop(0, chunks, own_step, zero)
    first = exchange(0)

    def same_cluster():
        row = train_ids[...].astype(jnp.float32)
        diagonal = (lax.broadcasted_iota(jnp.int32, (owned, owned), 0)
                    == lax.broadcasted_iota(jnp.int32, (owned, owned), 1))
        column = jnp.sum(jnp.where(diagonal, jnp.broadcast_to(row, (owned, owned)), 0.0), axis=1, keepdims=True)
        equal = []
        for step in range(STEPS):
            group = halves * query_rows
            source = lax.rem(blk + cycle - step, cycle)
            both = query_ids[:, pl.ds(pl.multiple_of(source * group, group), group)].astype(jnp.float32)
            keys = both[:, :query_rows]
            for h in range(1, halves):
                keys = jnp.where(half == h, both[:, h * query_rows:(h + 1) * query_rows], keys)
            equal.append(jnp.broadcast_to(column, (owned, query_rows)) == jnp.broadcast_to(keys, (owned, query_rows)))
        return equal

    equal = same_cluster()
    mine = pl.ds(pl.multiple_of(dim * owned, owned), owned)

    def finish(step, copies):
        total = partial[step, mine]
        for k, copy in enumerate(copies):
            copy.wait_recv()
            total = total + peers[step, k]
        out_ref[:, step * query_rows:(step + 1) * query_rows] = jnp.where(equal[step], 0.0, total)

    finish(0, first)

    def next_step(i, total):
        transfer(i).wait_send()

        @pl.when(i + flight < chunks)
        def _():
            transfer(i + flight).start()

        transfer(i).wait_recv()
        return score(columns_of(i), inbox[i], total)

    partial[1] = lax.fori_loop(0, chunks, next_step, zero)
    second = exchange(1)
    finish(1, second)
    for copy in first + second:
        copy.wait_send()


def solution(mesh):
    sizes = (mesh.shape["blk"], mesh.shape["dim"], mesh.shape["qs"])
    dims = sizes[1]

    def on_device(train_grads, query_grads, fisher, train_ids, query_ids):
        train_rows, depth = train_grads.shape
        query_rows = query_grads.shape[0]
        owned = train_ids.shape[0]
        chunks = depth // CHUNK
        out_shape = jax.ShapeDtypeStruct((owned, STEPS * query_rows), jnp.float32)
        return pl.pallas_call(
            functools.partial(kernel, sizes),
            out_shape=out_shape,
            in_specs=[pl.BlockSpec(memory_space=pltpu.HBM)] * 5,
            out_specs=pl.BlockSpec(memory_space=pltpu.VMEM),
            scratch_shapes=[
                pltpu.VMEM((train_rows, depth), train_grads.dtype),
                pltpu.VMEM((query_rows, depth), query_grads.dtype),
                pltpu.VMEM((chunks, query_rows, CHUNK), query_grads.dtype),
                pltpu.VMEM((1, depth), jnp.float32),
                pltpu.VMEM((1, owned), jnp.int32),
                pltpu.VMEM((1, query_ids.shape[0]), jnp.int32),
                pltpu.VMEM((STEPS, train_rows, query_rows), jnp.float32),
                pltpu.VMEM((STEPS, max(dims - 1, 1), owned, query_rows), jnp.float32),
                pltpu.SemaphoreType.DMA((chunks,)),
                pltpu.SemaphoreType.DMA((chunks,)),
                pltpu.SemaphoreType.DMA((5,)),
                pltpu.SemaphoreType.DMA((STEPS, max(dims - 1, 1))),
                pltpu.SemaphoreType.DMA((STEPS, max(dims - 1, 1))),
            ],
            cost_estimate=pl.CostEstimate(
                flops=4 * train_rows * query_rows * depth,
                bytes_accessed=2 * depth * (train_rows + 2 * query_rows), transcendentals=0),
            compiler_params=pltpu.CompilerParams(
                collective_id=0, has_side_effects=True, vmem_limit_bytes=60 << 20),
        )(train_grads, query_grads, fisher.reshape(1, -1), train_ids.reshape(1, -1), query_ids.reshape(1, -1))

    return jax.shard_map(
        on_device,
        mesh=mesh,
        in_specs=(
            P(("parts", "blk"), "dim"),
            P(("parts", "blk", "qs"), "dim"),
            P("dim"),
            P(("parts", "blk", "dim")),
            P("parts"),
        ),
        out_specs=P(("parts", "blk", "dim"), "qs"),
        check_vma=False,
    )
```

```python
import functools

import jax
import jax.numpy as jnp
from jax import lax
from jax.experimental import pallas as pl
from jax.experimental.pallas import tpu as pltpu
from jax.sharding import PartitionSpec as P

STEPS = 2
DAMPING = 0.1
CHUNK = 2048
IN_FLIGHT = 4
MESH = pl.DeviceIdType.MESH


def kernel(sizes, train_hbm, query_hbm, fisher_hbm, train_ids_hbm, query_ids_hbm, out_ref,
           train, own, inbox, scale, train_ids, query_ids, partial, peers,
           send_sem, recv_sem, load_sem, peer_send_sem, peer_recv_sem):
    cycle, dims, halves = sizes
    blk = lax.axis_index("blk")
    dim = lax.axis_index("dim")
    half = lax.axis_index("qs")
    after = lax.rem(blk + 1, cycle)
    before = lax.rem(blk + cycle - 1, cycle)
    train_rows = train.shape[0]
    query_rows, depth = own.shape
    owned = train_rows // dims
    chunks = depth // CHUNK

    def peer(k):
        return lax.rem(dim + k, dims)

    barrier = pltpu.get_barrier_semaphore()
    pl.semaphore_signal(barrier, inc=1, device_id={"blk": before}, device_id_type=MESH)
    for k in range(1, dims):
        pl.semaphore_signal(barrier, inc=1, device_id={"dim": peer(k)}, device_id_type=MESH)
    pl.semaphore_wait(barrier, dims)

    def transfer(i):
        return pltpu.make_async_remote_copy(
            src_ref=query_hbm.at[:, pl.ds(pl.multiple_of(i * CHUNK, CHUNK), CHUNK)],
            dst_ref=inbox.at[i],
            send_sem=send_sem.at[i],
            recv_sem=recv_sem.at[i],
            device_id={"blk": after},
            device_id_type=MESH,
        )

    flight = min(IN_FLIGHT, chunks)
    for i in range(flight):
        transfer(i).start()

    loads = [
        pltpu.make_async_copy(source, target, load_sem.at[n])
        for n, (source, target) in enumerate([
            (fisher_hbm, scale), (query_hbm, own), (train_hbm, train),
            (train_ids_hbm, train_ids), (query_ids_hbm, query_ids)])
    ]
    for load in loads:
        load.start()
    for load in loads:
        load.wait()

    scale[...] = 1.0 / (scale[...] + DAMPING)

    def score(columns, rows, total):
        scaled = (rows.astype(jnp.float32) * scale[:, columns]).astype(jnp.bfloat16)
        return total + lax.dot_general(
            train[:, columns], scaled, (((1,), (1,)), ((), ())), preferred_element_type=jnp.float32)

    def columns_of(i):
        return pl.ds(pl.multiple_of(i * CHUNK, CHUNK), CHUNK)

    zero = jnp.zeros((train_rows, query_rows), jnp.float32)

    def own_step(i, total):
        columns = columns_of(i)
        return score(columns, own[:, columns], total)

    def exchange(step):
        copies = []
        for k in range(1, dims):
            copies.append(pltpu.make_async_remote_copy(
                src_ref=partial.at[step, pl.ds(pl.multiple_of(peer(k) * owned, owned), owned)],
                dst_ref=peers.at[step, k - 1],
                send_sem=peer_send_sem.at[step, k - 1],
                recv_sem=peer_recv_sem.at[step, k - 1],
                device_id={"dim": peer(k)},
                device_id_type=MESH,
            ))
        for copy in copies:
            copy.start()
        return copies

    partial[0] = lax.fori_loop(0, chunks, own_step, zero)
    first = exchange(0)

    def same_cluster():
        row = train_ids[...].astype(jnp.float32)
        diagonal = (lax.broadcasted_iota(jnp.int32, (owned, owned), 0)
                    == lax.broadcasted_iota(jnp.int32, (owned, owned), 1))
        column = jnp.sum(jnp.where(diagonal, jnp.broadcast_to(row, (owned, owned)), 0.0), axis=1, keepdims=True)
        equal = []
        for step in range(STEPS):
            group = halves * query_rows
            source = lax.rem(blk + cycle - step, cycle)
            both = query_ids[:, pl.ds(pl.multiple_of(source * group, group), group)].astype(jnp.float32)
            keys = both[:, :query_rows]
            for h in range(1, halves):
                keys = jnp.where(half == h, both[:, h * query_rows:(h + 1) * query_rows], keys)
            equal.append(jnp.broadcast_to(column, (owned, query_rows)) == jnp.broadcast_to(keys, (owned, query_rows)))
        return equal

    equal = same_cluster()
    mine = pl.ds(pl.multiple_of(dim * owned, owned), owned)

    def finish(step, copies):
        total = partial[step, mine]
        for k, copy in enumerate(copies):
            copy.wait_recv()
            total = total + peers[step, k]
        out_ref[:, step * query_rows:(step + 1) * query_rows] = jnp.where(equal[step], 0.0, total)

    finish(0, first)

    def next_step(i, total):
        transfer(i).wait_send()

        @pl.when(i + flight < chunks)
        def _():
            transfer(i + flight).start()

        transfer(i).wait_recv()
        return score(columns_of(i), inbox[i], total)

    partial[1] = lax.fori_loop(0, chunks, next_step, zero)
    second = exchange(1)
    finish(1, second)
    for copy in first + second:
        copy.wait_send()


def solution(mesh):
    sizes = (mesh.shape["blk"], mesh.shape["dim"], mesh.shape["qs"])
    dims = sizes[1]

    def on_device(train_grads, query_grads, fisher, train_ids, query_ids):
        train_rows, depth = train_grads.shape
        query_rows = query_grads.shape[0]
        owned = train_ids.shape[0]
        chunks = depth // CHUNK
        out_shape = pltpu.VMEM((owned, STEPS * query_rows), jnp.float32)
        operands = [
            pltpu.with_memory_space_constraint(operand, pltpu.HBM)
            for operand in (train_grads, query_grads, fisher.reshape(1, -1),
                            train_ids.reshape(1, -1), query_ids.reshape(1, -1))
        ]
        return pl.pallas_call(
            functools.partial(kernel, sizes),
            out_shape=out_shape,
            in_specs=[pl.BlockSpec(memory_space=pltpu.HBM)] * 5,
            out_specs=pl.BlockSpec(memory_space=pltpu.VMEM),
            scratch_shapes=[
                pltpu.VMEM((train_rows, depth), train_grads.dtype),
                pltpu.VMEM((query_rows, depth), query_grads.dtype),
                pltpu.VMEM((chunks, query_rows, CHUNK), query_grads.dtype),
                pltpu.VMEM((1, depth), jnp.float32),
                pltpu.VMEM((1, owned), jnp.int32),
                pltpu.VMEM((1, query_ids.shape[0]), jnp.int32),
                pltpu.VMEM((STEPS, train_rows, query_rows), jnp.float32),
                pltpu.VMEM((STEPS, max(dims - 1, 1), owned, query_rows), jnp.float32),
                pltpu.SemaphoreType.DMA((chunks,)),
                pltpu.SemaphoreType.DMA((chunks,)),
                pltpu.SemaphoreType.DMA((5,)),
                pltpu.SemaphoreType.DMA((STEPS, max(dims - 1, 1))),
                pltpu.SemaphoreType.DMA((STEPS, max(dims - 1, 1))),
            ],
            cost_estimate=pl.CostEstimate(
                flops=4 * train_rows * query_rows * depth,
                bytes_accessed=2 * depth * (train_rows + 2 * query_rows), transcendentals=0),
            compiler_params=pltpu.CompilerParams(
                collective_id=0, has_side_effects=True, vmem_limit_bytes=48 << 20),
        )(*operands)

    return jax.shard_map(
        on_device,
        mesh=mesh,
        in_specs=(
            P(("parts", "blk"), "dim"),
            P(("parts", "blk", "qs"), "dim"),
            P("dim"),
            P(("parts", "blk", "dim")),
            P("parts"),
        ),
        out_specs=P(("parts", "blk", "dim"), "qs"),
        check_vma=False,
    )
```

```python
import functools

import jax
import jax.numpy as jnp
from jax import lax
from jax.experimental import pallas as pl
from jax.experimental.pallas import tpu as pltpu
from jax.sharding import PartitionSpec as P

STEPS = 2
DAMPING = 0.1
CHUNK = 2048
NARROW = 2
MESH = pl.DeviceIdType.MESH


def kernel(sizes, train_hbm, query_hbm, fisher_hbm, train_ids_hbm, query_ids_hbm, out_ref,
           train, own, inbox, scale, train_ids, query_ids, partial, peers,
           send_sem, recv_sem, load_sem, peer_send_sem, peer_recv_sem):
    cycle, dims, halves = sizes
    blk = lax.axis_index("blk")
    dim = lax.axis_index("dim")
    half = lax.axis_index("qs")
    after = lax.rem(blk + 1, cycle)
    before = lax.rem(blk + cycle - 1, cycle)
    train_rows = train.shape[0]
    query_rows, depth = own.shape
    owned = train_rows // dims
    chunks = depth // CHUNK

    def peer(k):
        return lax.rem(dim + k, dims)

    barrier = pltpu.get_barrier_semaphore()
    pl.semaphore_signal(barrier, inc=1, device_id={"blk": before}, device_id_type=MESH)
    for k in range(1, dims):
        pl.semaphore_signal(barrier, inc=1, device_id={"dim": peer(k)}, device_id_type=MESH)
    pl.semaphore_wait(barrier, dims)

    def transfer(i):
        return pltpu.make_async_remote_copy(
            src_ref=query_hbm.at[:, pl.ds(pl.multiple_of(i * CHUNK, CHUNK), CHUNK)],
            dst_ref=inbox.at[i],
            send_sem=send_sem.at[i],
            recv_sem=recv_sem.at[i],
            device_id={"blk": after},
            device_id_type=MESH,
        )

    narrow = min(NARROW, chunks)
    flight = jnp.where(half == 0, chunks, narrow)
    for i in range(narrow):
        transfer(i).start()

    @pl.when(half == 0)
    def _():
        for i in range(narrow, chunks):
            transfer(i).start()

    loads = [
        pltpu.make_async_copy(source, target, load_sem.at[n])
        for n, (source, target) in enumerate([
            (fisher_hbm, scale), (query_hbm, own), (train_hbm, train),
            (train_ids_hbm, train_ids), (query_ids_hbm, query_ids)])
    ]
    for load in loads:
        load.start()
    for load in loads:
        load.wait()

    scale[...] = 1.0 / (scale[...] + DAMPING)

    def score(columns, rows, total):
        scaled = (rows.astype(jnp.float32) * scale[:, columns]).astype(jnp.bfloat16)
        return total + lax.dot_general(
            train[:, columns], scaled, (((1,), (1,)), ((), ())), preferred_element_type=jnp.float32)

    def columns_of(i):
        return pl.ds(pl.multiple_of(i * CHUNK, CHUNK), CHUNK)

    zero = jnp.zeros((train_rows, query_rows), jnp.float32)

    def own_step(i, total):
        columns = columns_of(i)
        return score(columns, own[:, columns], total)

    def exchange(step):
        copies = []
        for k in range(1, dims):
            copies.append(pltpu.make_async_remote_copy(
                src_ref=partial.at[step, pl.ds(pl.multiple_of(peer(k) * owned, owned), owned)],
                dst_ref=peers.at[step, k - 1],
                send_sem=peer_send_sem.at[step, k - 1],
                recv_sem=peer_recv_sem.at[step, k - 1],
                device_id={"dim": peer(k)},
                device_id_type=MESH,
            ))
        for copy in copies:
            copy.start()
        return copies

    partial[0] = lax.fori_loop(0, chunks, own_step, zero)
    first = exchange(0)

    def same_cluster():
        row = train_ids[...].astype(jnp.float32)
        diagonal = (lax.broadcasted_iota(jnp.int32, (owned, owned), 0)
                    == lax.broadcasted_iota(jnp.int32, (owned, owned), 1))
        column = jnp.sum(jnp.where(diagonal, jnp.broadcast_to(row, (owned, owned)), 0.0), axis=1, keepdims=True)
        equal = []
        for step in range(STEPS):
            group = halves * query_rows
            source = lax.rem(blk + cycle - step, cycle)
            both = query_ids[:, pl.ds(pl.multiple_of(source * group, group), group)].astype(jnp.float32)
            keys = both[:, :query_rows]
            for h in range(1, halves):
                keys = jnp.where(half == h, both[:, h * query_rows:(h + 1) * query_rows], keys)
            equal.append(jnp.broadcast_to(column, (owned, query_rows)) == jnp.broadcast_to(keys, (owned, query_rows)))
        return equal

    equal = same_cluster()
    mine = pl.ds(pl.multiple_of(dim * owned, owned), owned)

    def finish(step, copies):
        total = partial[step, mine]
        for k, copy in enumerate(copies):
            copy.wait_recv()
            total = total + peers[step, k]
        out_ref[:, step * query_rows:(step + 1) * query_rows] = jnp.where(equal[step], 0.0, total)

    finish(0, first)

    def next_step(i, total):
        transfer(i).wait_send()

        @pl.when(i + flight < chunks)
        def _():
            transfer(i + flight).start()

        transfer(i).wait_recv()
        return score(columns_of(i), inbox[i], total)

    partial[1] = lax.fori_loop(0, chunks, next_step, zero)
    second = exchange(1)
    finish(1, second)
    for copy in first + second:
        copy.wait_send()


def solution(mesh):
    sizes = (mesh.shape["blk"], mesh.shape["dim"], mesh.shape["qs"])
    dims = sizes[1]

    def on_device(train_grads, query_grads, fisher, train_ids, query_ids):
        train_rows, depth = train_grads.shape
        query_rows = query_grads.shape[0]
        owned = train_ids.shape[0]
        chunks = depth // CHUNK
        out_shape = pltpu.VMEM((owned, STEPS * query_rows), jnp.float32)
        operands = [
            pltpu.with_memory_space_constraint(operand, pltpu.HBM)
            for operand in (train_grads, query_grads, fisher.reshape(1, -1),
                            train_ids.reshape(1, -1), query_ids.reshape(1, -1))
        ]
        return pl.pallas_call(
            functools.partial(kernel, sizes),
            out_shape=out_shape,
            in_specs=[pl.BlockSpec(memory_space=pltpu.HBM)] * 5,
            out_specs=pl.BlockSpec(memory_space=pltpu.VMEM),
            scratch_shapes=[
                pltpu.VMEM((train_rows, depth), train_grads.dtype),
                pltpu.VMEM((query_rows, depth), query_grads.dtype),
                pltpu.VMEM((chunks, query_rows, CHUNK), query_grads.dtype),
                pltpu.VMEM((1, depth), jnp.float32),
                pltpu.VMEM((1, owned), jnp.int32),
                pltpu.VMEM((1, query_ids.shape[0]), jnp.int32),
                pltpu.VMEM((STEPS, train_rows, query_rows), jnp.float32),
                pltpu.VMEM((STEPS, max(dims - 1, 1), owned, query_rows), jnp.float32),
                pltpu.SemaphoreType.DMA((chunks,)),
                pltpu.SemaphoreType.DMA((chunks,)),
                pltpu.SemaphoreType.DMA((5,)),
                pltpu.SemaphoreType.DMA((STEPS, max(dims - 1, 1))),
                pltpu.SemaphoreType.DMA((STEPS, max(dims - 1, 1))),
            ],
            cost_estimate=pl.CostEstimate(
                flops=4 * train_rows * query_rows * depth,
                bytes_accessed=2 * depth * (train_rows + 2 * query_rows), transcendentals=0),
            compiler_params=pltpu.CompilerParams(
                collective_id=0, has_side_effects=True, vmem_limit_bytes=48 << 20),
        )(*operands)

    return jax.shard_map(
        on_device,
        mesh=mesh,
        in_specs=(
            P(("parts", "blk"), "dim"),
            P(("parts", "blk", "qs"), "dim"),
            P("dim"),
            P(("parts", "blk", "dim")),
            P("parts"),
        ),
        out_specs=P(("parts", "blk", "dim"), "qs"),
        check_vma=False,
    )
```

```python
import functools

import jax
import jax.numpy as jnp
from jax import lax
from jax.experimental import pallas as pl
from jax.experimental.pallas import tpu as pltpu
from jax.sharding import PartitionSpec as P

STEPS = 2
DAMPING = 0.1
CHUNK = 4096
NARROW = 1
MESH = pl.DeviceIdType.MESH


def kernel(sizes, train_hbm, query_hbm, fisher_hbm, train_ids_hbm, query_ids_hbm, out_ref,
           train, own, inbox, scale, train_ids, query_ids, partial, peers,
           send_sem, recv_sem, load_sem, peer_send_sem, peer_recv_sem):
    cycle, dims, halves = sizes
    blk = lax.axis_index("blk")
    dim = lax.axis_index("dim")
    half = lax.axis_index("qs")
    after = lax.rem(blk + 1, cycle)
    before = lax.rem(blk + cycle - 1, cycle)
    train_rows = train.shape[0]
    query_rows, depth = own.shape
    owned = train_rows // dims
    chunks = depth // CHUNK

    def peer(k):
        return lax.rem(dim + k, dims)

    barrier = pltpu.get_barrier_semaphore()
    pl.semaphore_signal(barrier, inc=1, device_id={"blk": before}, device_id_type=MESH)
    for k in range(1, dims):
        pl.semaphore_signal(barrier, inc=1, device_id={"dim": peer(k)}, device_id_type=MESH)
    pl.semaphore_wait(barrier, dims)

    def transfer(i):
        return pltpu.make_async_remote_copy(
            src_ref=query_hbm.at[:, pl.ds(pl.multiple_of(i * CHUNK, CHUNK), CHUNK)],
            dst_ref=inbox.at[i],
            send_sem=send_sem.at[i],
            recv_sem=recv_sem.at[i],
            device_id={"blk": after},
            device_id_type=MESH,
        )

    narrow = min(NARROW, chunks)
    flight = jnp.where(half == 0, chunks, narrow)
    for i in range(narrow):
        transfer(i).start()

    @pl.when(half == 0)
    def _():
        for i in range(narrow, chunks):
            transfer(i).start()

    loads = [
        pltpu.make_async_copy(source, target, load_sem.at[n])
        for n, (source, target) in enumerate([
            (fisher_hbm, scale), (query_hbm, own), (train_hbm, train),
            (train_ids_hbm, train_ids), (query_ids_hbm, query_ids)])
    ]
    for load in loads:
        load.start()
    for load in loads:
        load.wait()

    scale[...] = 1.0 / (scale[...] + DAMPING)

    def score(columns, rows, total):
        scaled = (rows.astype(jnp.float32) * scale[:, columns]).astype(jnp.bfloat16)
        return total + lax.dot_general(
            train[:, columns], scaled, (((1,), (1,)), ((), ())), preferred_element_type=jnp.float32)

    def columns_of(i):
        return pl.ds(pl.multiple_of(i * CHUNK, CHUNK), CHUNK)

    zero = jnp.zeros((train_rows, query_rows), jnp.float32)

    def own_step(i, total):
        columns = columns_of(i)
        return score(columns, own[:, columns], total)

    def exchange(step):
        copies = []
        for k in range(1, dims):
            copies.append(pltpu.make_async_remote_copy(
                src_ref=partial.at[step, pl.ds(pl.multiple_of(peer(k) * owned, owned), owned)],
                dst_ref=peers.at[step, k - 1],
                send_sem=peer_send_sem.at[step, k - 1],
                recv_sem=peer_recv_sem.at[step, k - 1],
                device_id={"dim": peer(k)},
                device_id_type=MESH,
            ))
        for copy in copies:
            copy.start()
        return copies

    partial[0] = lax.fori_loop(0, chunks, own_step, zero)
    first = exchange(0)

    def same_cluster():
        row = train_ids[...].astype(jnp.float32)
        diagonal = (lax.broadcasted_iota(jnp.int32, (owned, owned), 0)
                    == lax.broadcasted_iota(jnp.int32, (owned, owned), 1))
        column = jnp.sum(jnp.where(diagonal, jnp.broadcast_to(row, (owned, owned)), 0.0), axis=1, keepdims=True)
        equal = []
        for step in range(STEPS):
            group = halves * query_rows
            source = lax.rem(blk + cycle - step, cycle)
            both = query_ids[:, pl.ds(pl.multiple_of(source * group, group), group)].astype(jnp.float32)
            keys = both[:, :query_rows]
            for h in range(1, halves):
                keys = jnp.where(half == h, both[:, h * query_rows:(h + 1) * query_rows], keys)
            equal.append(jnp.broadcast_to(column, (owned, query_rows)) == jnp.broadcast_to(keys, (owned, query_rows)))
        return equal

    equal = same_cluster()
    mine = pl.ds(pl.multiple_of(dim * owned, owned), owned)

    def finish(step, copies):
        total = partial[step, mine]
        for k, copy in enumerate(copies):
            copy.wait_recv()
            total = total + peers[step, k]
        out_ref[:, step * query_rows:(step + 1) * query_rows] = jnp.where(equal[step], 0.0, total)

    finish(0, first)

    def next_step(i, total):
        transfer(i).wait_send()

        @pl.when(i + flight < chunks)
        def _():
            transfer(i + flight).start()

        transfer(i).wait_recv()
        return score(columns_of(i), inbox[i], total)

    partial[1] = lax.fori_loop(0, chunks, next_step, zero)
    second = exchange(1)
    finish(1, second)
    for copy in first + second:
        copy.wait_send()


def solution(mesh):
    sizes = (mesh.shape["blk"], mesh.shape["dim"], mesh.shape["qs"])
    dims = sizes[1]

    def on_device(train_grads, query_grads, fisher, train_ids, query_ids):
        train_rows, depth = train_grads.shape
        query_rows = query_grads.shape[0]
        owned = train_ids.shape[0]
        chunks = depth // CHUNK
        out_shape = pltpu.VMEM((owned, STEPS * query_rows), jnp.float32)
        operands = [
            pltpu.with_memory_space_constraint(operand, pltpu.HBM)
            for operand in (train_grads, query_grads, fisher.reshape(1, -1),
                            train_ids.reshape(1, -1), query_ids.reshape(1, -1))
        ]
        return pl.pallas_call(
            functools.partial(kernel, sizes),
            out_shape=out_shape,
            in_specs=[pl.BlockSpec(memory_space=pltpu.HBM)] * 5,
            out_specs=pl.BlockSpec(memory_space=pltpu.VMEM),
            scratch_shapes=[
                pltpu.VMEM((train_rows, depth), train_grads.dtype),
                pltpu.VMEM((query_rows, depth), query_grads.dtype),
                pltpu.VMEM((chunks, query_rows, CHUNK), query_grads.dtype),
                pltpu.VMEM((1, depth), jnp.float32),
                pltpu.VMEM((1, owned), jnp.int32),
                pltpu.VMEM((1, query_ids.shape[0]), jnp.int32),
                pltpu.VMEM((STEPS, train_rows, query_rows), jnp.float32),
                pltpu.VMEM((STEPS, max(dims - 1, 1), owned, query_rows), jnp.float32),
                pltpu.SemaphoreType.DMA((chunks,)),
                pltpu.SemaphoreType.DMA((chunks,)),
                pltpu.SemaphoreType.DMA((5,)),
                pltpu.SemaphoreType.DMA((STEPS, max(dims - 1, 1))),
                pltpu.SemaphoreType.DMA((STEPS, max(dims - 1, 1))),
            ],
            cost_estimate=pl.CostEstimate(
                flops=4 * train_rows * query_rows * depth,
                bytes_accessed=2 * depth * (train_rows + 2 * query_rows), transcendentals=0),
            compiler_params=pltpu.CompilerParams(
                collective_id=0, has_side_effects=True, vmem_limit_bytes=48 << 20),
        )(*operands)

    return jax.shard_map(
        on_device,
        mesh=mesh,
        in_specs=(
            P(("parts", "blk"), "dim"),
            P(("parts", "blk", "qs"), "dim"),
            P("dim"),
            P(("parts", "blk", "dim")),
            P("parts"),
        ),
        out_specs=P(("parts", "blk", "dim"), "qs"),
        check_vma=False,
    )
```
